32 devices in a mesh: src: 8 (over z, core), rcv: 2 (over y), int: 2 (over x).
Axes of the slice: x: 2, y: 2, z: 4, core: 2. Of those that a mesh axis runs over, the one named last changes fastest.
Arguments:
- traces: float32 [2, 1, 4096, 4096], P(None, None, 'src', 'rcv'), may hold values from -6 to 6
- missing: int32 [32, 32], P('src', 'rcv'), may hold values from 0 to 1, as said below
- aperture: int32 [32, 24], P('src'), may hold values from 0 to 32, as said below
- wavelet: float32 [2, 1], replicated, may hold values from -0.06 to 0.06
Outputs:
- primaries: float32 [2, 1, 4096, 4096], P(None, None, 'src', ('rcv', 'int'))
The draws below stay inside these ranges and needn't reach their ends.
Inputs may be any that keep to these rules, and one draw needn't show every extreme that they name: `missing`: A tile is marked only where its receiver block lies above its source block, so the mirrored tile is always recorded; some tile is marked. `aperture`: in each row the listed blocks come first and are distinct; the remaining entries are the padding value 32. Each row lists 24 // 2 to 24 blocks; some row lists exactly 24 and some row exactly 12.
All inputs are finite; a program needn't handle non-finite values.
Results may differ from the reference program's by a relative error of at most 0.00005.
Values sent between devices are 32-bit elements; how exact they have to be, the bound alone decides.
A program may use at most 128 MiB of HBM per device.

```python
import jax
import jax.numpy as jnp
from jax import lax

GRID = 4096
TILE = 128
APER = 24
NFREQ = 1


def draw_missing(key, part):
    block_count = GRID // TILE
    coins = jax.random.randint(jax.random.fold_in(key, 11), (block_count, block_count), 0, 3)
    upper = jnp.arange(block_count)[None, :] > jnp.arange(block_count)[:, None]
    marks = jnp.where((coins == 0) & upper, 1, 0).astype(jnp.int32)
    return marks.at[0, block_count - 1].set(1)


def draw_aperture(key, part):
    block_count = GRID // TILE
    row_keys = jax.random.split(jax.random.fold_in(key, 23), block_count)
    orders = jax.vmap(lambda one_key: jax.random.permutation(one_key, block_count))(row_keys).astype(jnp.int32)
    counts = jax.random.randint(jax.random.fold_in(key, 37), (block_count,), APER // 2, APER + 1)
    counts = counts.at[0].set(APER).at[block_count - 1].set(APER // 2)
    slots = jnp.arange(APER)[None, :]
    return jnp.where(slots < counts[:, None], orders[:, :APER], block_count).astype(jnp.int32)


def block_scale(own_key, shape, pieces, least, high):
    level, own = 1.0, jax.random.fold_in(own_key, 6)
    for position, blocks in pieces:
        draws = jnp.exp(jax.random.uniform(jax.random.fold_in(own, position), (blocks,), jnp.float32, least / len(pieces), high / len(pieces)))
        level = level * jnp.repeat(draws, shape[position] // blocks).reshape([-1 if axis == position else 1 for axis in range(len(shape))])
    return level


def centred(own_key, extent, scale, most, pieces=(), kind=jnp.bfloat16):
    gain = block_scale(own_key, extent, pieces, -0.22, 0.18) if pieces else 1.0
    entries = jax.random.normal(own_key, extent, jnp.float32) * scale * gain
    return jnp.minimum(jnp.maximum(entries, -most), most).astype(kind)


def setup_inputs(seed: int = 0) -> dict:
    keys = jax.random.split(jax.random.key(seed), 5)
    traces = centred(keys[0], (2, NFREQ, GRID, GRID), 1.0, 6.0, ((2, 8), (3, 2)), jnp.float32)
    missing = draw_missing(jax.random.fold_in(keys[4], 71), 0)
    aperture = draw_aperture(jax.random.fold_in(keys[4], 71), 0)
    wavelet = centred(keys[3], (2, NFREQ), 0.0125, 0.06, (), jnp.float32)
    return dict(traces=traces, missing=missing, aperture=aperture, wavelet=wavelet)


def complex_prod(left_side, right_side):
    return jnp.einsum("fik,fkj->fij", left_side, right_side, precision=lax.Precision.HIGHEST)


def reference(traces, missing, aperture, wavelet):
    block_count = GRID // TILE
    mirrored = jnp.swapaxes(traces, 2, 3)
    tile_mask = jnp.repeat(jnp.repeat(missing, TILE, axis=0), TILE, axis=1) > 0
    filled = jnp.where(tile_mask[None, None], mirrored, traces)
    chosen = (aperture[:, :, None] == jnp.arange(block_count, dtype=jnp.int32)[None, None, :]).astype(jnp.float32).sum(axis=1)
    chosen_full = jnp.repeat(jnp.repeat(chosen, TILE, axis=0), TILE, axis=1)
    weighted = filled * chosen_full[None, None]
    pred_real = complex_prod(weighted[0], filled[0]) - complex_prod(weighted[1], filled[1])
    pred_imag = complex_prod(weighted[0], filled[1]) + complex_prod(weighted[1], filled[0])
    w_real = wavelet[0][:, None, None]
    w_imag = wavelet[1][:, None, None]
    out_real = filled[0] - (w_real * pred_real - w_imag * pred_imag)
    out_imag = filled[1] - (w_real * pred_imag + w_imag * pred_real)
    return jnp.stack([out_real, out_imag])
```

```python
import jax
import jax.numpy as jnp
from jax import lax
from jax.sharding import PartitionSpec as P

TILE = 128
EVERY = ("src", "rcv", "int")


def product(left_side, right_side):
    return jnp.dot(left_side, right_side, precision=lax.Precision.HIGH)


def mirror_pairs(src_count, rcv_count, int_count, half):
    col_count = rcv_count * int_count
    pairs = []
    for s in range(src_count):
        for q in range(col_count):
            if s >= 2 * q + half:
                pairs.append((s * col_count + q, (2 * q + half) * col_count + s // 2))
    return pairs


def per_device(traces, missing, aperture, wavelet):
    src_count, rcv_count, int_count = (lax.axis_size(a) for a in EVERY)
    col_count = rcv_count * int_count
    assert src_count == 2 * col_count
    rows, wide = traces.shape[2], traces.shape[3]
    cols = wide // int_count
    my_int = lax.axis_index("int")
    s = lax.axis_index("src")
    own = lax.dynamic_slice_in_dim(traces[:, 0], my_int * cols, cols, axis=2)
    arrived = []
    for half in (0, 1):
        part = own[:, :, half * rows : (half + 1) * rows]
        for sender in (0, 1):
            pairs = [
                (a, b)
                for a, b in mirror_pairs(src_count, rcv_count, int_count, half)
                if (a // col_count) % 2 == sender
            ]
            arrived.append(lax.ppermute(part, EVERY, pairs))
    odd = (s % 2) == 1
    first = jnp.where(odd, arrived[2], arrived[0])
    second = jnp.where(odd, arrived[3], arrived[1])
    mirrored = jnp.concatenate([jnp.swapaxes(first, 1, 2), jnp.swapaxes(second, 1, 2)], axis=2)
    row_tiles, col_tiles = rows // TILE, cols // TILE
    my_missing = lax.dynamic_slice_in_dim(missing, my_int * col_tiles, col_tiles, axis=1)
    mask = jnp.repeat(jnp.repeat(my_missing > 0, TILE, axis=0), TILE, axis=1)
    filled = jnp.where(mask[None], mirrored, own)
    left = lax.all_gather(filled, ("rcv", "int"), axis=0)
    right = lax.all_gather(filled, "src", axis=1, tiled=True)
    blocks = col_count * col_tiles
    chosen = (
        (aperture[:, :, None] == jnp.arange(blocks, dtype=jnp.int32)[None, None, :])
        .astype(jnp.float32)
        .sum(axis=1)
    )
    scale = jnp.repeat(jnp.repeat(chosen, TILE, axis=0), TILE, axis=1)
    left = jnp.moveaxis(left, 0, 2).reshape(2, rows, col_count * cols) * scale[None]
    first_prod = product(left[0], right[0])
    second_prod = product(left[1], right[1])
    third_prod = product(left[0] + left[1], right[0] + right[1])
    real = first_prod - second_prod
    imag = third_prod - first_prod - second_prod
    w_real, w_imag = wavelet[0, 0], wavelet[1, 0]
    out_real = filled[0] - (w_real * real - w_imag * imag)
    out_imag = filled[1] - (w_real * imag + w_imag * real)
    return jnp.stack([out_real, out_imag])[:, None]


def solution(mesh):
    placed = (P(None, None, "src", "rcv"), P("src", "rcv"), P("src", None), P())
    return jax.shard_map(
        per_device,
        mesh=mesh,
        in_specs=placed,
        out_specs=P(None, None, "src", ("rcv", "int")),
        check_vma=False,
    )
```

```python
import functools

import jax
import jax.numpy as jnp
from jax import lax
from jax.experimental import pallas as pl
from jax.experimental.pallas import tpu as pltpu
from jax.sharding import PartitionSpec as P

TILE = 128
EVERY = ("src", "rcv", "int")
MESH = pl.DeviceIdType.MESH
LAG_FILL = 2
LAG_MOVE = 3


def product(left_side, right_side):
    return jnp.dot(left_side, right_side, precision=lax.Precision.HIGH)


def gather_kernel(sizes, own, mask, right, left, turned, kept, recv, recv_turn, sent, local):
    layers, int_count, rows, edge = sizes
    na = rows // edge
    nb = 2 * na
    rounds = na * nb
    s = lax.axis_index("src")
    z, c = s // 2, s % 2
    q = lax.axis_index("rcv") * int_count + lax.axis_index("int")

    def device(layer, core, column):
        return {"src": 2 * layer + core, "rcv": column // int_count, "int": column % int_count}

    def straight(r):
        a, rest = r // nb, r % nb
        return a, na * (rest % 2) + rest // 2

    def mirrored(r):
        a, rest = r // nb, r % nb
        return rest // 2, na * (rest % 2) + a

    def place(layer, column, r):
        (a0, b0), (a1, b1) = straight(r), mirrored(r)
        raw = jnp.where(layer > column, 1, 0)
        return a0 * raw + a1 * (1 - raw), b0 * raw + b1 * (1 - raw)

    def span(index, base=0):
        return pl.ds(pl.multiple_of(base + index * edge, edge), edge)

    def in_right(layer, core, a, b):
        return right.at[:, span(a, (2 * layer + core) * rows), span(b)]

    DOWN, UP, SIDE, ROW, TURN = range(5)

    def remote(source, target, kind, j, r, where, sem=None):
        return pltpu.make_async_remote_copy(
            src_ref=source,
            dst_ref=target,
            send_sem=sent.at[kind, j, r],
            recv_sem=recv.at[kind, j, r] if sem is None else sem,
            device_id=where,
            device_id_type=MESH,
        )

    def move(kind, j, r, source):
        a, b = place(j, q, r)
        where = {DOWN: (z - 1, c), UP: (z + 1, c), SIDE: (z, 1 - c)}[kind]
        source = in_right(j, c, a, b) if source is None else source.at[:, span(a), span(b)]
        return remote(source, in_right(j, c, a, b), kind, j, r, device(*where, q))

    def arrival(kind, j, core, r):
        a, b = place(j, q, r)
        ref = in_right(j, core, a, b)
        return remote(ref, ref, kind, j, r, device(z, 1 - c, q))

    def row_send(other, r):
        a, b = place(z, q, r)
        return remote(
            kept.at[:, span(a), span(b)], left.at[q, :, span(a), span(b)], ROW, other, r, device(z, c, other),
            recv.at[ROW, q, r],
        )

    def row_arrival(other, r):
        a, b = place(z, other, r)
        ref = left.at[other, :, span(a), span(b)]
        return remote(ref, ref, ROW, other, r, device(z, 1 - c, q))

    def turn_parts(j, r, source):
        a, b = straight(r)
        core = b // na
        slot = a * nb + 2 * (b % na) + c
        ref = in_right(j, c, a, b) if source is None else source.at[:, span(a), span(b)]
        return ref, core, slot

    def turn(j, r, source):
        ref, core, slot = turn_parts(j, r, source)
        return remote(ref, turned.at[slot], TURN, j, r, device(z, core, j), recv_turn.at[slot])

    def turn_here(r):
        ref, _, slot = turn_parts(z, r, own)
        return pltpu.make_async_copy(ref, turned.at[slot], recv_turn.at[slot])

    def keep(which, r):
        a, b = place(z, q, r)
        target = in_right(z, c, a, b) if which == 0 else left.at[q, :, span(a), span(b)]
        return pltpu.make_async_copy(kept.at[:, span(a), span(b)], target, local.at[which, r])

    def turn_arrival(f):
        return pltpu.make_async_copy(turned.at[f], turned.at[f], recv_turn.at[f])

    barrier = pltpu.get_barrier_semaphore()

    def greet(layer, core, column):
        pl.semaphore_signal(barrier, inc=1, device_id=device(layer, core, column), device_id_type=MESH)

    for column in range(layers):
        greet(z, 1 - c, column)

        @pl.when(column != q)
        def _():
            greet(z, c, column)

    @pl.when(z > 0)
    def _():
        greet(z - 1, c, q)

    @pl.when(z < layers - 1)
    def _():
        greet(z + 1, c, q)

    ends = jnp.where(z > 0, 1, 0) + jnp.where(z < layers - 1, 1, 0)
    pl.semaphore_wait(barrier, 2 * layers - 1 + ends)

    def own_moves(r, do):
        @pl.when(z > 0)
        def _():
            do(move(DOWN, z, r, kept))

        @pl.when(z < layers - 1)
        def _():
            do(move(UP, z, r, kept))

        do(move(SIDE, z, r, kept))
        for other in range(layers):

            @pl.when(other != q)
            def _():
                do(row_send(other, r))

    def start(copy):
        copy.start()

    def own_round(r):
        a, b = place(z, q, r)

        @pl.when(z > q)
        def _():
            kept[:, span(a), span(b)] = own[:, span(a), span(b)]

        @pl.when(z <= q)
        def _():
            turn_arrival(r).wait()
            per = edge // TILE
            for comp in range(2):
                flipped = turned[r, comp].T
                for i in range(per):
                    row = pl.ds(pl.multiple_of(a * edge + i * TILE, TILE), TILE)
                    marks = mask[pl.ds(pl.multiple_of((a * per + i) * 8, 8), 1), span(b)]
                    part = flipped[i * TILE : (i + 1) * TILE]
                    kept[comp, row, span(b)] = jnp.where(marks > 0.5, part, own[comp, row, span(b)])

        own_moves(r, start)
        keep(0, r).start()
        keep(1, r).start()

    def pass_on(j, r, do, waiting):
        @pl.when(z < j)
        def _():
            if waiting:
                arrival(DOWN, j, c, r).wait_recv()

            @pl.when(z > 0)
            def _():
                do(move(DOWN, j, r, None))

            @pl.when(q == z)
            def _():
                do(turn(j, r, None))

        @pl.when(z > j)
        def _():
            if waiting:
                arrival(UP, j, c, r).wait_recv()

            @pl.when(z < layers - 1)
            def _():
                do(move(UP, j, r, None))

        @pl.when(z != j)
        def _():
            do(move(SIDE, j, r, None))

    def first_turn(r, _):
        @pl.when(straight(r)[1] // na == c)
        def _():
            turn_here(r).start()

        @pl.when(straight(r)[1] // na != c)
        def _():
            turn(z, r, own).start()

        return 0

    @pl.when(q == z)
    def _():
        lax.fori_loop(0, rounds, first_turn, 0)

    def step(t, _):
        @pl.when((t < rounds) & (z > q))
        def _():
            own_round(t)

        @pl.when(t < rounds)
        def _():
            for j in range(layers):

                @pl.when(j > q)
                def _():
                    pass_on(j, t, start, True)

        @pl.when((t >= LAG_FILL) & (t < rounds + LAG_FILL) & (z <= q))
        def _():
            own_round(t - LAG_FILL)

        @pl.when(t >= LAG_MOVE)
        def _():
            for j in range(layers):

                @pl.when(j <= q)
                def _():
                    pass_on(j, t - LAG_MOVE, start, True)

        return 0

    lax.fori_loop(0, rounds + LAG_MOVE, step, 0)

    def done(copy):
        copy.wait_send()

    def finish(r, _):
        own_moves(r, done)
        keep(0, r).wait()
        keep(1, r).wait()
        for j in range(layers):
            pass_on(j, r, done, False)
            arrival(SIDE, j, 1 - c, r).wait_recv()

            @pl.when(j != q)
            def _():
                row_arrival(j, r).wait_recv()

        @pl.when((q == z) & (straight(r)[1] // na != c))
        def _():
            turn(z, r, own).wait_send()

        return 0

    lax.fori_loop(0, rounds, finish, 0)


def gather_panels(own, mask, layers, int_count):
    rows = own.shape[1]
    edge = max(TILE, rows // 2)
    rounds = 2 * (rows // edge) ** 2
    return pl.pallas_call(
        functools.partial(gather_kernel, (layers, int_count, rows, edge)),
        out_shape=(
            jax.ShapeDtypeStruct((2, 2 * layers * rows, 2 * rows), jnp.float32),
            jax.ShapeDtypeStruct((layers, 2, rows, 2 * rows), jnp.float32),
        ),
        in_specs=[pl.BlockSpec(memory_space=pltpu.VMEM)] * 2,
        out_specs=[pl.BlockSpec(memory_space=pl.ANY)] * 2,
        scratch_shapes=[
            pltpu.VMEM((rounds, 2, edge, edge), jnp.float32),
            pltpu.VMEM((2, rows, 2 * rows), jnp.float32),
            pltpu.SemaphoreType.DMA((4, layers, rounds)),
            pltpu.SemaphoreType.DMA((rounds,)),
            pltpu.SemaphoreType.DMA((5, layers, rounds)),
            pltpu.SemaphoreType.DMA((2, rounds)),
        ],
        compiler_params=pltpu.CompilerParams(
            collective_id=0, has_side_effects=True, vmem_limit_bytes=40 * 2**20
        ),
    )(own, mask)


def per_device(traces, missing, aperture, wavelet):
    src_count, rcv_count, int_count = (lax.axis_size(a) for a in EVERY)
    col_count = rcv_count * int_count
    assert src_count == 2 * col_count
    rows, wide = traces.shape[2], traces.shape[3]
    cols = wide // int_count
    my_int = lax.axis_index("int")
    s = lax.axis_index("src")
    own = lax.dynamic_slice_in_dim(traces[:, 0], my_int * cols, cols, axis=2)
    row_tiles, col_tiles = rows // TILE, cols // TILE
    my_missing = lax.dynamic_slice_in_dim(missing, my_int * col_tiles, col_tiles, axis=1)
    mask = jnp.repeat(jnp.repeat((my_missing > 0).astype(jnp.float32), 8, axis=0), TILE, axis=1)
    right, left = gather_panels(own, mask, col_count, int_count)
    filled = lax.dynamic_slice_in_dim(right, s * rows, rows, axis=1)
    blocks = col_count * col_tiles
    chosen = (
        (aperture[:, :, None] == jnp.arange(blocks, dtype=jnp.int32)[None, None, :])
        .astype(jnp.float32)
        .sum(axis=1)
    )
    scale = jnp.repeat(jnp.repeat(chosen, TILE, axis=0), TILE, axis=1)
    left = jnp.moveaxis(left, 0, 2).reshape(2, rows, col_count * cols) * scale[None]
    first_prod = product(left[0], right[0])
    second_prod = product(left[1], right[1])
    third_prod = product(left[0] + left[1], right[0] + right[1])
    real = first_prod - second_prod
    imag = third_prod - first_prod - second_prod
    w_real, w_imag = wavelet[0, 0], wavelet[1, 0]
    out_real = filled[0] - (w_real * real - w_imag * imag)
    out_imag = filled[1] - (w_real * imag + w_imag * real)
    return jnp.stack([out_real, out_imag])[:, None]


def solution(mesh):
    placed = (P(None, None, "src", "rcv"), P("src", "rcv"), P("src", None), P())
    return jax.shard_map(
        per_device,
        mesh=mesh,
        in_specs=placed,
        out_specs=P(None, None, "src", ("rcv", "int")),
        check_vma=False,
    )
```

```python
import functools

import jax
import jax.numpy as jnp
from jax import lax
from jax.experimental import pallas as pl
from jax.experimental.pallas import tpu as pltpu
from jax.sharding import PartitionSpec as P

TILE = 128
EVERY = ("src", "rcv", "int")
MESH = pl.DeviceIdType.MESH
LAG_FILL = 4
LAG_MOVE = 6


def split(value):
    high = value.astype(jnp.bfloat16)
    return high, (value - high.astype(jnp.float32)).astype(jnp.bfloat16)


def three_pass(left_parts, right_parts):
    (lh, ll), (rh, rl) = left_parts, right_parts
    dot = functools.partial(jnp.dot, preferred_element_type=jnp.float32)
    return dot(lh, rh) + (dot(lh, rl) + dot(ll, rh))


def predict_kernel(left, right, scale, kept, wavelet, out, total):
    step = pl.program_id(1)

    @pl.when(step == 0)
    def _():
        total[...] = jnp.zeros_like(total)

    weights = scale[...]
    lr, li = left[0] * weights, left[1] * weights
    fr, fi = right[0], right[1]
    first = three_pass(split(lr), split(fr))
    second = three_pass(split(li), split(fi))
    total[0] += first - second
    total[1] += three_pass(split(lr + li), split(fr + fi)) - (first + second)

    @pl.when(step == pl.num_programs(1) - 1)
    def _():
        wr, wi = wavelet[0, 0], wavelet[1, 0]
        out[0] = kept[0] - (wr * total[0] - wi * total[1])
        out[1] = kept[1] - (wr * total[1] + wi * total[0])


def predict(left, right, scale, wavelet, place):
    blocks, _, rows, wide = left.shape
    cols = right.shape[2]
    deep = min(wide, 512)
    per = wide // deep
    width = min(cols, 512)
    return pl.pallas_call(
        predict_kernel,
        grid=(cols // width, blocks * per),
        in_specs=[
            pl.BlockSpec((None, 2, rows, deep), lambda n, k: (k // per, 0, 0, k % per)),
            pl.BlockSpec((2, deep, width), lambda n, k: (0, k, n)),
            pl.BlockSpec((rows, deep), lambda n, k: (0, k)),
            pl.BlockSpec((2, rows, width), lambda n, k: (0, 0, n)),
            pl.BlockSpec(memory_space=pltpu.SMEM),
        ],
        out_specs=pl.BlockSpec((2, rows, width), lambda n, k: (0, 0, n)),
        out_shape=jax.ShapeDtypeStruct((2, rows, cols), jnp.float32),
        scratch_shapes=[pltpu.VMEM((2, rows, width), jnp.float32)],
        compiler_params=pltpu.CompilerParams(vmem_limit_bytes=56 * 2**20),
    )(left, right, scale, place, wavelet)


def gather_kernel(sizes, own, mask, right, left, turned, kept, recv, recv_turn, sent, local):
    layers, int_count, rows, edge = sizes
    na = rows // edge
    nb = 2 * na
    rounds = na * nb
    s = lax.axis_index("src")
    z, c = s // 2, s % 2
    y, x = lax.axis_index("rcv"), lax.axis_index("int")
    q = y * int_count + x

    def device(layer, core, column):
        return {"src": 2 * layer + core, "rcv": column // int_count, "int": column % int_count}

    def straight(r):
        a, rest = r // nb, r % nb
        return a, na * (rest % 2) + rest // 2

    def mirrored(r):
        a, rest = r // nb, r % nb
        return rest // 2, na * (rest % 2) + a

    def place(layer, column, r):
        (a0, b0), (a1, b1) = straight(r), mirrored(r)
        raw = jnp.where(layer > column, 1, 0)
        return a0 * raw + a1 * (1 - raw), b0 * raw + b1 * (1 - raw)

    def span(index, base=0):
        return pl.ds(pl.multiple_of(base + index * edge, edge), edge)

    def in_right(layer, core, a, b):
        return right.at[:, span(a, (2 * layer + core) * rows), span(b)]

    DOWN, UP, SIDE, ROW, TURN, RELAY = range(6)

    def remote(source, target, kind, j, r, where, sem=None):
        return pltpu.make_async_remote_copy(
            src_ref=source,
            dst_ref=target,
            send_sem=sent.at[kind, j, r],
            recv_sem=recv.at[kind, j, r] if sem is None else sem,
            device_id=where,
            device_id_type=MESH,
        )

    def move(kind, j, r, source):
        a, b = place(j, q, r)
        where = {DOWN: (z - 1, c), UP: (z + 1, c), SIDE: (z, 1 - c)}[kind]
        source = in_right(j, c, a, b) if source is None else source.at[:, span(a), span(b)]
        return remote(source, in_right(j, c, a, b), kind, j, r, device(*where, q))

    def arrival(kind, j, core, r):
        a, b = place(j, q, r)
        ref = in_right(j, core, a, b)
        return remote(ref, ref, kind, j, r, device(z, 1 - c, q))

    def row_send(other, r):
        a, b = place(z, q, r)
        return remote(
            kept.at[:, span(a), span(b)], left.at[q, :, span(a), span(b)], ROW, other, r, device(z, c, other),
            recv.at[ROW, q, r],
        )

    def row_arrival(other, r):
        a, b = place(z, other, r)
        ref = left.at[other, :, span(a), span(b)]
        return remote(ref, ref, ROW, other, r, device(z, 1 - c, q))

    def relays(r, do, waiting):
        for other in range(layers):

            @pl.when((other != q) & (other % int_count == x))
            def _():
                if waiting:
                    row_arrival(other, r).wait_recv()
                a, b = place(z, other, r)
                ref = left.at[other, :, span(a), span(b)]
                for x2 in range(int_count):

                    @pl.when(x2 != x)
                    def _():
                        to = (other // int_count) * int_count + x2
                        where = device(z, c, y * int_count + x2)
                        do(remote(ref, ref, RELAY, to, r, where, recv.at[ROW, other, r]))

    def turn_parts(j, r, source):
        a, b = straight(r)
        core = b // na
        slot = a * nb + 2 * (b % na) + c
        ref = in_right(j, c, a, b) if source is None else source.at[:, span(a), span(b)]
        return ref, core, slot

    def turn(j, r, source):
        ref, core, slot = turn_parts(j, r, source)
        return remote(ref, turned.at[slot], TURN, j, r, device(z, core, j), recv_turn.at[slot])

    def turn_here(r):
        ref, _, slot = turn_parts(z, r, own)
        return pltpu.make_async_copy(ref, turned.at[slot], recv_turn.at[slot])

    def keep(which, r):
        a, b = place(z, q, r)
        target = in_right(z, c, a, b) if which == 0 else left.at[q, :, span(a), span(b)]
        return pltpu.make_async_copy(kept.at[:, span(a), span(b)], target, local.at[which, r])

    def turn_arrival(f):
        return pltpu.make_async_copy(turned.at[f], turned.at[f], recv_turn.at[f])

    barrier = pltpu.get_barrier_semaphore()

    def greet(layer, core, column):
        pl.semaphore_signal(barrier, inc=1, device_id=device(layer, core, column), device_id_type=MESH)

    for column in range(layers):
        greet(z, 1 - c, column)

        @pl.when(column != q)
        def _():
            greet(z, c, column)

    @pl.when(z > 0)
    def _():
        greet(z - 1, c, q)

    @pl.when(z < layers - 1)
    def _():
        greet(z + 1, c, q)

    ends = jnp.where(z > 0, 1, 0) + jnp.where(z < layers - 1, 1, 0)
    pl.semaphore_wait(barrier, 2 * layers - 1 + ends)

    def own_moves(r, do):
        @pl.when(z > 0)
        def _():
            do(move(DOWN, z, r, kept))

        @pl.when(z < layers - 1)
        def _():
            do(move(UP, z, r, kept))

        do(move(SIDE, z, r, kept))
        for other in range(layers):

            @pl.when((other != q) & ((other % int_count == x) | (other // int_count == y)))
            def _():
                do(row_send(other, r))

    def start(copy):
        copy.start()

    def own_round(r):
        a, b = place(z, q, r)

        @pl.when(z > q)
        def _():
            kept[:, span(a), span(b)] = own[:, span(a), span(b)]

        @pl.when(z <= q)
        def _():
            turn_arrival(r).wait()
            per = edge // TILE
            for comp in range(2):
                flipped = turned[r, comp].T
                for i in range(per):
                    row = pl.ds(pl.multiple_of(a * edge + i * TILE, TILE), TILE)
                    marks = mask[pl.ds(pl.multiple_of((a * per + i) * 8, 8), 1), span(b)]
                    part = flipped[i * TILE : (i + 1) * TILE]
                    kept[comp, row, span(b)] = jnp.where(marks > 0.5, part, own[comp, row, span(b)])

        own_moves(r, start)
        keep(0, r).start()
        keep(1, r).start()

    def pass_on(j, r, do, waiting):
        @pl.when(z < j)
        def _():
            if waiting:
                arrival(DOWN, j, c, r).wait_recv()

            @pl.when(z > 0)
            def _():
                do(move(DOWN, j, r, None))

            @pl.when(q == z)
            def _():
                do(turn(j, r, None))

        @pl.when(z > j)
        def _():
            if waiting:
                arrival(UP, j, c, r).wait_recv()

            @pl.when(z < layers - 1)
            def _():
                do(move(UP, j, r, None))

        @pl.when(z != j)
        def _():
            do(move(SIDE, j, r, None))

    def first_turn(r, _):
        @pl.when(straight(r)[1] // na == c)
        def _():
            turn_here(r).start()

        @pl.when(straight(r)[1] // na != c)
        def _():
            turn(z, r, own).start()

        return 0

    @pl.when(q == z)
    def _():
        lax.fori_loop(0, rounds, first_turn, 0)

    def step(t, _):
        @pl.when((t < rounds) & (z > q))
        def _():
            own_round(t)

        @pl.when(t < rounds)
        def _():
            for j in range(layers):

                @pl.when(j > q)
                def _():
                    pass_on(j, t, start, True)

        @pl.when((t >= LAG_FILL) & (t < rounds + LAG_FILL) & (z <= q))
        def _():
            own_round(t - LAG_FILL)

        @pl.when(t >= LAG_MOVE)
        def _():
            for j in range(layers):

                @pl.when(j <= q)
                def _():
                    pass_on(j, t - LAG_MOVE, start, True)

            relays(t - LAG_MOVE, start, True)

        return 0

    lax.fori_loop(0, rounds + LAG_MOVE, step, 0)

    def done(copy):
        copy.wait_send()

    def finish(r, _):
        own_moves(r, done)
        relays(r, done, False)
        keep(0, r).wait()
        keep(1, r).wait()
        for j in range(layers):
            pass_on(j, r, done, False)
            arrival(SIDE, j, 1 - c, r).wait_recv()

            @pl.when((j != q) & (j % int_count != x))
            def _():
                row_arrival(j, r).wait_recv()

        @pl.when((q == z) & (straight(r)[1] // na != c))
        def _():
            turn(z, r, own).wait_send()

        return 0

    lax.fori_loop(0, rounds, finish, 0)


def gather_panels(own, mask, layers, int_count):
    rows = own.shape[1]
    edge = max(TILE, rows // 4)
    rounds = 2 * (rows // edge) ** 2
    return pl.pallas_call(
        functools.partial(gather_kernel, (layers, int_count, rows, edge)),
        out_shape=(
            jax.ShapeDtypeStruct((2, 2 * layers * rows, 2 * rows), jnp.float32),
            jax.ShapeDtypeStruct((layers, 2, rows, 2 * rows), jnp.float32),
        ),
        in_specs=[pl.BlockSpec(memory_space=pltpu.VMEM)] * 2,
        out_specs=[pl.BlockSpec(memory_space=pl.ANY)] * 2,
        scratch_shapes=[
            pltpu.VMEM((rounds, 2, edge, edge), jnp.float32),
            pltpu.VMEM((2, rows, 2 * rows), jnp.float32),
            pltpu.SemaphoreType.DMA((4, layers, rounds)),
            pltpu.SemaphoreType.DMA((rounds,)),
            pltpu.SemaphoreType.DMA((6, layers, rounds)),
            pltpu.SemaphoreType.DMA((2, rounds)),
        ],
        compiler_params=pltpu.CompilerParams(
            collective_id=0, has_side_effects=True, vmem_limit_bytes=40 * 2**20
        ),
    )(own, mask)


def per_device(traces, missing, aperture, wavelet):
    src_count, rcv_count, int_count = (lax.axis_size(a) for a in EVERY)
    col_count = rcv_count * int_count
    assert src_count == 2 * col_count
    rows, wide = traces.shape[2], traces.shape[3]
    cols = wide // int_count
    my_int = lax.axis_index("int")
    s = lax.axis_index("src")
    own = lax.dynamic_slice_in_dim(traces[:, 0], my_int * cols, cols, axis=2)
    row_tiles, col_tiles = rows // TILE, cols // TILE
    my_missing = lax.dynamic_slice_in_dim(missing, my_int * col_tiles, col_tiles, axis=1)
    mask = jnp.repeat(jnp.repeat((my_missing > 0).astype(jnp.float32), 8, axis=0), TILE, axis=1)
    right, left = gather_panels(own, mask, col_count, int_count)
    filled = lax.dynamic_slice_in_dim(right, s * rows, rows, axis=1)
    blocks = col_count * col_tiles
    chosen = (
        (aperture[:, :, None] == jnp.arange(blocks, dtype=jnp.int32)[None, None, :])
        .astype(jnp.float32)
        .sum(axis=1)
    )
    scale = jnp.repeat(jnp.repeat(chosen, TILE, axis=0), TILE, axis=1)
    return predict(left, right, scale, wavelet, filled)[:, None]


def solution(mesh):
    placed = (P(None, None, "src", "rcv"), P("src", "rcv"), P("src", None), P())
    return jax.shard_map(
        per_device,
        mesh=mesh,
        in_specs=placed,
        out_specs=P(None, None, "src", ("rcv", "int")),
        check_vma=False,
    )
```

```python
import functools

import jax
import jax.numpy as jnp
from jax import lax
from jax.experimental import pallas as pl
from jax.experimental.pallas import tpu as pltpu
from jax.sharding import PartitionSpec as P

TILE = 128
EVERY = ("src", "rcv", "int")
MESH = pl.DeviceIdType.MESH
LAG_FILL = 2
LAG_MOVE = 3


def split(value):
    high = value.astype(jnp.bfloat16)
    return high, (value - high.astype(jnp.float32)).astype(jnp.bfloat16)


def three_pass(left_parts, right_parts):
    (lh, ll), (rh, rl) = left_parts, right_parts
    dot = functools.partial(jnp.dot, preferred_element_type=jnp.float32)
    return dot(lh, rh) + (dot(lh, rl) + dot(ll, rh))


def predict_kernel(my_block, left, right, chosen, kept, wavelet, out, total):
    step = pl.program_id(1)
    na, _, _, edge, _ = left.shape
    nb = right.shape[1]
    per = edge // TILE

    @pl.when(step == 0)
    def _():
        total[...] = jnp.zeros_like(total)

    def weighted(comp):
        bands = []
        for a in range(na):
            for i in range(per):
                tiles = []
                for b in range(na):
                    for k in range(per):
                        tile = left[a, b, comp, i * TILE : (i + 1) * TILE, k * TILE : (k + 1) * TILE]
                        tiles.append(tile * chosen[a * per + i, (step * na + b) * per + k])
                bands.append(jnp.concatenate(tiles, axis=1))
        return jnp.concatenate(bands, axis=0)

    def panel(comp):
        bands = [jnp.concatenate([right[a, b, comp] for b in range(nb)], axis=1) for a in range(na)]
        return jnp.concatenate(bands, axis=0)

    lr, li = weighted(0), weighted(1)
    fr, fi = panel(0), panel(1)
    first = three_pass(split(lr), split(fr))
    second = three_pass(split(li), split(fi))
    total[0] += first - second
    total[1] += three_pass(split(lr + li), split(fr + fi)) - (first + second)

    @pl.when(step == pl.num_programs(1) - 1)
    def _():
        wr, wi = wavelet[0, 0], wavelet[1, 0]
        for a in range(na):
            for b in range(nb):
                at = (slice(a * edge, (a + 1) * edge), slice(b * edge, (b + 1) * edge))
                real, imag = total[0, *at], total[1, *at]
                out[0, *at] = kept[a, b, 0] - (wr * real - wi * imag)
                out[1, *at] = kept[a, b, 1] - (wr * imag + wi * real)


def predict(left, right, chosen, wavelet, my_block, na):
    columns, rounds, _, edge, _ = left.shape
    blocks = right.shape[0]
    nb = rounds // na
    left = left.reshape(columns, na, nb, 2, edge, edge)
    right = right.reshape(blocks, na, nb, 2, edge, edge)
    rows, cols = na * edge, nb * edge
    width = min(cols, 512)
    some = width // edge
    panel = (None, na, some, 2, edge, edge)
    return pl.pallas_call(
        predict_kernel,
        grid_spec=pltpu.PrefetchScalarGridSpec(
            num_scalar_prefetch=1,
            grid=(cols // width, blocks),
            in_specs=[
                pl.BlockSpec((None, na, na, 2, edge, edge), lambda n, k, s: (k // 2, 0, k % 2, 0, 0, 0)),
                pl.BlockSpec(panel, lambda n, k, s: (k, 0, n, 0, 0, 0)),
                pl.BlockSpec(memory_space=pltpu.SMEM),
                pl.BlockSpec(panel, lambda n, k, s: (s[0], 0, n, 0, 0, 0)),
                pl.BlockSpec(memory_space=pltpu.SMEM),
            ],
            out_specs=pl.BlockSpec((2, rows, width), lambda n, k, s: (0, 0, n)),
            scratch_shapes=[pltpu.VMEM((2, rows, width), jnp.float32)],
        ),
        out_shape=jax.ShapeDtypeStruct((2, rows, cols), jnp.float32),
        compiler_params=pltpu.CompilerParams(vmem_limit_bytes=56 * 2**20),
    )(my_block, left, right, chosen, right, wavelet)


def gather_kernel(sizes, own, mask, right, left, turned, kept, recv, recv_turn, sent, local):
    layers, int_count, rows, edge = sizes
    na = rows // edge
    nb = 2 * na
    rounds = na * nb
    s = lax.axis_index("src")
    z, c = s // 2, s % 2
    y, x = lax.axis_index("rcv"), lax.axis_index("int")
    q = y * int_count + x

    def device(layer, core, column):
        return {"src": 2 * layer + core, "rcv": column // int_count, "int": column % int_count}

    def straight(r):
        a, rest = r // nb, r % nb
        return a, na * (rest % 2) + rest // 2

    def mirrored(r):
        a, rest = r // nb, r % nb
        return rest // 2, na * (rest % 2) + a

    def place(layer, column, r):
        (a0, b0), (a1, b1) = straight(r), mirrored(r)
        raw = jnp.where(layer > column, 1, 0)
        return a0 * raw + a1 * (1 - raw), b0 * raw + b1 * (1 - raw)

    def in_right(layer, core, a, b):
        return right.at[2 * layer + core, a * nb + b]

    DOWN, UP, SIDE, ROW, TURN, RELAY = range(6)

    def remote(source, target, kind, j, r, where, sem=None):
        return pltpu.make_async_remote_copy(
            src_ref=source,
            dst_ref=target,
            send_sem=sent.at[kind, j, r],
            recv_sem=recv.at[kind, j, r] if sem is None else sem,
            device_id=where,
            device_id_type=MESH,
        )

    def move(kind, j, r, source):
        a, b = place(j, q, r)
        where = {DOWN: (z - 1, c), UP: (z + 1, c), SIDE: (z, 1 - c)}[kind]
        source = in_right(j, c, a, b) if source is None else source.at[a * nb + b]
        return remote(source, in_right(j, c, a, b), kind, j, r, device(*where, q))

    def arrival(kind, j, core, r):
        a, b = place(j, q, r)
        ref = in_right(j, core, a, b)
        return remote(ref, ref, kind, j, r, device(z, 1 - c, q))

    def row_send(other, r):
        a, b = place(z, q, r)
        return remote(
            kept.at[a * nb + b], left.at[q, a * nb + b], ROW, other, r, device(z, c, other),
            recv.at[ROW, q, r],
        )

    def row_arrival(other, r):
        a, b = place(z, other, r)
        ref = left.at[other, a * nb + b]
        return remote(ref, ref, ROW, other, r, device(z, 1 - c, q))

    def relays(r, do, waiting):
        for other in range(layers):

            @pl.when((other != q) & (other % int_count == x))
            def _():
                if waiting:
                    row_arrival(other, r).wait_recv()
                a, b = place(z, other, r)
                ref = left.at[other, a * nb + b]
                for x2 in range(int_count):

                    @pl.when(x2 != x)
                    def _():
                        to = (other // int_count) * int_count + x2
                        where = device(z, c, y * int_count + x2)
                        do(remote(ref, ref, RELAY, to, r, where, recv.at[ROW, other, r]))

    def turn_parts(j, r, source):
        a, b = straight(r)
        core = b // na
        slot = a * nb + 2 * (b % na) + c
        ref = in_right(j, c, a, b) if source is None else source.at[a * nb + b]
        return ref, core, slot

    def turn(j, r, source):
        ref, core, slot = turn_parts(j, r, source)
        return remote(ref, turned.at[slot], TURN, j, r, device(z, core, j), recv_turn.at[slot])

    def turn_here(r):
        ref, _, slot = turn_parts(z, r, own)
        return pltpu.make_async_copy(ref, turned.at[slot], recv_turn.at[slot])

    def keep(which, r):
        a, b = place(z, q, r)
        target = in_right(z, c, a, b) if which == 0 else left.at[q, a * nb + b]
        return pltpu.make_async_copy(kept.at[a * nb + b], target, local.at[which, r])

    def turn_arrival(f):
        return pltpu.make_async_copy(turned.at[f], turned.at[f], recv_turn.at[f])

    barrier = pltpu.get_barrier_semaphore()

    def greet(layer, core, column):
        pl.semaphore_signal(barrier, inc=1, device_id=device(layer, core, column), device_id_type=MESH)

    for column in range(layers):
        greet(z, 1 - c, column)

        @pl.when(column != q)
        def _():
            greet(z, c, column)

    @pl.when(z > 0)
    def _():
        greet(z - 1, c, q)

    @pl.when(z < layers - 1)
    def _():
        greet(z + 1, c, q)

    ends = jnp.where(z > 0, 1, 0) + jnp.where(z < layers - 1, 1, 0)
    pl.semaphore_wait(barrier, 2 * layers - 1 + ends)

    def own_moves(r, do):
        @pl.when(z > 0)
        def _():
            do(move(DOWN, z, r, kept))

        @pl.when(z < layers - 1)
        def _():
            do(move(UP, z, r, kept))

        do(move(SIDE, z, r, kept))
        for other in range(layers):

            @pl.when((other != q) & ((other % int_count == x) | (other // int_count == y)))
            def _():
                do(row_send(other, r))

    def start(copy):
        copy.start()

    def own_round(r):
        a, b = place(z, q, r)

        square = a * nb + b

        @pl.when(z > q)
        def _():
            kept[square] = own[square]

        @pl.when(z <= q)
        def _():
            turn_arrival(r).wait()
            per = edge // TILE
            lanes = pl.ds(pl.multiple_of(b * edge, edge), edge)
            for comp in range(2):
                flipped = turned[r, comp].T
                for i in range(per):
                    row = slice(i * TILE, (i + 1) * TILE)
                    marks = mask[pl.ds(pl.multiple_of((a * per + i) * 8, 8), 1), lanes]
                    kept[square, comp, row] = jnp.where(marks > 0.5, flipped[row], own[square, comp, row])

        own_moves(r, start)
        keep(0, r).start()
        keep(1, r).start()

    def pass_on(j, r, do, waiting):
        @pl.when(z < j)
        def _():
            if waiting:
                arrival(DOWN, j, c, r).wait_recv()

            @pl.when(z > 0)
            def _():
                do(move(DOWN, j, r, None))

            @pl.when(q == z)
            def _():
                do(turn(j, r, None))

        @pl.when(z > j)
        def _():
            if waiting:
                arrival(UP, j, c, r).wait_recv()

            @pl.when(z < layers - 1)
            def _():
                do(move(UP, j, r, None))

        @pl.when(z != j)
        def _():
            do(move(SIDE, j, r, None))

    def first_turn(r, _):
        @pl.when(straight(r)[1] // na == c)
        def _():
            turn_here(r).start()

        @pl.when(straight(r)[1] // na != c)
        def _():
            turn(z, r, own).start()

        return 0

    @pl.when(q == z)
    def _():
        lax.fori_loop(0, rounds, first_turn, 0)

    def step(t, _):
        @pl.when((t < rounds) & (z > q))
        def _():
            own_round(t)

        @pl.when(t < rounds)
        def _():
            for j in range(layers):

                @pl.when(j > q)
                def _():
                    pass_on(j, t, start, True)

        @pl.when((t >= LAG_FILL) & (t < rounds + LAG_FILL) & (z <= q))
        def _():
            own_round(t - LAG_FILL)

        @pl.when(t >= LAG_MOVE)
        def _():
            for j in range(layers):

                @pl.when(j <= q)
                def _():
                    pass_on(j, t - LAG_MOVE, start, True)

            relays(t - LAG_MOVE, start, True)

        return 0

    lax.fori_loop(0, rounds + LAG_MOVE, step, 0)

    def done(copy):
        copy.wait_send()

    def finish(r, _):
        own_moves(r, done)
        relays(r, done, False)
        keep(0, r).wait()
        keep(1, r).wait()
        for j in range(layers):
            pass_on(j, r, done, False)
            arrival(SIDE, j, 1 - c, r).wait_recv()

            @pl.when((j != q) & (j % int_count != x))
            def _():
                row_arrival(j, r).wait_recv()

        @pl.when((q == z) & (straight(r)[1] // na != c))
        def _():
            turn(z, r, own).wait_send()

        return 0

    lax.fori_loop(0, rounds, finish, 0)


def gather_panels(own, mask, layers, int_count):
    rounds, _, edge, _ = own.shape
    rows = edge * int((rounds // 2) ** 0.5)
    return pl.pallas_call(
        functools.partial(gather_kernel, (layers, int_count, rows, edge)),
        out_shape=(
            jax.ShapeDtypeStruct((2 * layers, *own.shape), jnp.float32),
            jax.ShapeDtypeStruct((layers, *own.shape), jnp.float32),
        ),
        in_specs=[pl.BlockSpec(memory_space=pltpu.VMEM)] * 2,
        out_specs=[pl.BlockSpec(memory_space=pl.ANY)] * 2,
        scratch_shapes=[
            pltpu.VMEM(own.shape, jnp.float32),
            pltpu.VMEM(own.shape, jnp.float32),
            pltpu.SemaphoreType.DMA((4, layers, rounds)),
            pltpu.SemaphoreType.DMA((rounds,)),
            pltpu.SemaphoreType.DMA((6, layers, rounds)),
            pltpu.SemaphoreType.DMA((2, rounds)),
        ],
        compiler_params=pltpu.CompilerParams(
            collective_id=0, has_side_effects=True, vmem_limit_bytes=40 * 2**20
        ),
    )(own, mask)


def per_device(traces, missing, aperture, wavelet):
    src_count, rcv_count, int_count = (lax.axis_size(a) for a in EVERY)
    col_count = rcv_count * int_count
    assert src_count == 2 * col_count
    rows, wide = traces.shape[2], traces.shape[3]
    cols = wide // int_count
    my_int = lax.axis_index("int")
    s = lax.axis_index("src")
    own = lax.dynamic_slice_in_dim(traces[:, 0], my_int * cols, cols, axis=2)
    row_tiles, col_tiles = rows // TILE, cols // TILE
    my_missing = lax.dynamic_slice_in_dim(missing, my_int * col_tiles, col_tiles, axis=1)
    mask = jnp.repeat(jnp.repeat((my_missing > 0).astype(jnp.float32), 8, axis=0), TILE, axis=1)
    edge = max(TILE, rows // 2)
    na = rows // edge
    own = jnp.stack(
        [own[:, a * edge : (a + 1) * edge, b * edge : (b + 1) * edge] for a in range(na) for b in range(2 * na)]
    )
    right, left = gather_panels(own, mask, col_count, int_count)
    blocks = col_count * col_tiles
    chosen = (
        (aperture[:, :, None] == jnp.arange(blocks, dtype=jnp.int32)[None, None, :])
        .astype(jnp.float32)
        .sum(axis=1)
    )
    return predict(left, right, chosen, wavelet, s.reshape(1), na)[:, None]


def solution(mesh):
    placed = (P(None, None, "src", "rcv"), P("src", "rcv"), P("src", None), P())
    return jax.shard_map(
        per_device,
        mesh=mesh,
        in_specs=placed,
        out_specs=P(None, None, "src", ("rcv", "int")),
        check_vma=False,
    )
```

```python
import functools

import jax
import jax.numpy as jnp
from jax import lax
from jax.experimental import pallas as pl
from jax.experimental.pallas import tpu as pltpu
from jax.sharding import PartitionSpec as P

TILE = 128
EVERY = ("src", "rcv", "int")
MESH = pl.DeviceIdType.MESH
LAG_FILL = 4
LAG_MOVE = 7


def split(value):
    high = value.astype(jnp.bfloat16)
    return high, (value - high.astype(jnp.float32)).astype(jnp.bfloat16)


def three_pass(left_parts, right_parts):
    (lh, ll), (rh, rl) = left_parts, right_parts
    dot = functools.partial(jnp.dot, preferred_element_type=jnp.float32)
    return dot(lh, rh) + (dot(lh, rl) + dot(ll, rh))


def predict_kernel(my_block, left, right, chosen, kept, wavelet, out, total):
    step = pl.program_id(1)
    na, _, _, edge, _ = left.shape
    nb = right.shape[1]
    per = edge // TILE

    @pl.when(step == 0)
    def _():
        total[...] = jnp.zeros_like(total)

    def weighted(comp):
        bands = []
        for a in range(na):
            for i in range(per):
                tiles = []
                for b in range(na):
                    for k in range(per):
                        tile = left[a, b, comp, i * TILE : (i + 1) * TILE, k * TILE : (k + 1) * TILE]
                        tiles.append(tile * chosen[a * per + i, (step * na + b) * per + k])
                bands.append(jnp.concatenate(tiles, axis=1))
        return jnp.concatenate(bands, axis=0)

    def panel(comp):
        bands = [jnp.concatenate([right[a, b, comp] for b in range(nb)], axis=1) for a in range(na)]
        return jnp.concatenate(bands, axis=0)

    lr, li = weighted(0), weighted(1)
    fr, fi = panel(0), panel(1)
    first = three_pass(split(lr), split(fr))
    second = three_pass(split(li), split(fi))
    total[0] += first - second
    total[1] += three_pass(split(lr + li), split(fr + fi)) - (first + second)

    @pl.when(step == pl.num_programs(1) - 1)
    def _():
        wr, wi = wavelet[0, 0], wavelet[1, 0]
        for a in range(na):
            for b in range(nb):
                at = (slice(a * edge, (a + 1) * edge), slice(b * edge, (b + 1) * edge))
                real, imag = total[0, *at], total[1, *at]
                out[0, *at] = kept[a, b, 0] - (wr * real - wi * imag)
                out[1, *at] = kept[a, b, 1] - (wr * imag + wi * real)


def predict(left, right, chosen, wavelet, my_block, na):
    columns, rounds, _, edge, _ = left.shape
    blocks = right.shape[0]
    nb = rounds // na
    left = left.reshape(columns, na, nb, 2, edge, edge)
    right = right.reshape(blocks, na, nb, 2, edge, edge)
    rows, cols = na * edge, nb * edge
    width = min(cols, 512)
    some = width // edge
    panel = (None, na, some, 2, edge, edge)
    return pl.pallas_call(
        predict_kernel,
        grid_spec=pltpu.PrefetchScalarGridSpec(
            num_scalar_prefetch=1,
            grid=(cols // width, blocks),
            in_specs=[
                pl.BlockSpec((None, na, na, 2, edge, edge), lambda n, k, s: (k // 2, 0, k % 2, 0, 0, 0)),
                pl.BlockSpec(panel, lambda n, k, s: (k, 0, n, 0, 0, 0)),
                pl.BlockSpec(memory_space=pltpu.SMEM),
                pl.BlockSpec(panel, lambda n, k, s: (s[0], 0, n, 0, 0, 0)),
                pl.BlockSpec(memory_space=pltpu.SMEM),
            ],
            out_specs=pl.BlockSpec((2, rows, width), lambda n, k, s: (0, 0, n)),
            scratch_shapes=[pltpu.VMEM((2, rows, width), jnp.float32)],
        ),
        out_shape=jax.ShapeDtypeStruct((2, rows, cols), jnp.float32),
        compiler_params=pltpu.CompilerParams(vmem_limit_bytes=56 * 2**20),
    )(my_block, left, right, chosen, right, wavelet)


def gather_kernel(sizes, own, mask, right, left, turned, kept, recv, recv_turn, sent, local):
    layers, int_count, rows, edge = sizes
    na = rows // edge
    nb = 2 * na
    rounds = na * nb
    s = lax.axis_index("src")
    z, c = s // 2, s % 2
    y, x = lax.axis_index("rcv"), lax.axis_index("int")
    q = y * int_count + x

    def device(layer, core, column):
        return {"src": 2 * layer + core, "rcv": column // int_count, "int": column % int_count}

    def straight(r):
        a, rest = r // nb, r % nb
        return a, na * (rest % 2) + rest // 2

    def mirrored(r):
        a, rest = r // nb, r % nb
        return rest // 2, na * (rest % 2) + a

    def place(layer, column, r):
        (a0, b0), (a1, b1) = straight(r), mirrored(r)
        raw = jnp.where(layer > column, 1, 0)
        return a0 * raw + a1 * (1 - raw), b0 * raw + b1 * (1 - raw)

    def in_right(layer, core, a, b):
        return right.at[2 * layer + core, a * nb + b]

    DOWN, UP, SIDE, ROW, TURN, RELAY = range(6)

    def remote(source, target, kind, j, r, where, sem=None):
        return pltpu.make_async_remote_copy(
            src_ref=source,
            dst_ref=target,
            send_sem=sent.at[kind, j, r],
            recv_sem=recv.at[kind, j, r] if sem is None else sem,
            device_id=where,
            device_id_type=MESH,
        )

    def move(kind, j, r, source):
        a, b = place(j, q, r)
        where = {DOWN: (z - 1, c), UP: (z + 1, c), SIDE: (z, 1 - c)}[kind]
        source = in_right(j, c, a, b) if source is None else source.at[a * nb + b]
        return remote(source, in_right(j, c, a, b), kind, j, r, device(*where, q))

    def arrival(kind, j, core, r):
        a, b = place(j, q, r)
        ref = in_right(j, core, a, b)
        return remote(ref, ref, kind, j, r, device(z, 1 - c, q))

    def row_send(other, r):
        a, b = place(z, q, r)
        return remote(
            kept.at[a * nb + b], left.at[q, a * nb + b], ROW, other, r, device(z, c, other),
            recv.at[ROW, q, r],
        )

    def row_arrival(other, r):
        a, b = place(z, other, r)
        ref = left.at[other, a * nb + b]
        return remote(ref, ref, ROW, other, r, device(z, 1 - c, q))

    def relays(r, do, waiting):
        for other in range(layers):

            @pl.when((other != q) & (other % int_count == x))
            def _():
                if waiting:
                    row_arrival(other, r).wait_recv()
                a, b = place(z, other, r)
                ref = left.at[other, a * nb + b]
                for x2 in range(int_count):

                    @pl.when(x2 != x)
                    def _():
                        to = (other // int_count) * int_count + x2
                        where = device(z, c, y * int_count + x2)
                        do(remote(ref, ref, RELAY, to, r, where, recv.at[ROW, other, r]))

    def turn_parts(j, r, source):
        a, b = straight(r)
        core = b // na
        slot = a * nb + 2 * (b % na) + c
        ref = in_right(j, c, a, b) if source is None else source.at[a * nb + b]
        return ref, core, slot

    def turn(j, r, source):
        ref, core, slot = turn_parts(j, r, source)
        return remote(ref, turned.at[slot], TURN, j, r, device(z, core, j), recv_turn.at[slot])

    def turn_here(r):
        ref, _, slot = turn_parts(z, r, own)
        return pltpu.make_async_copy(ref, turned.at[slot], recv_turn.at[slot])

    def keep(which, r):
        a, b = place(z, q, r)
        target = in_right(z, c, a, b) if which == 0 else left.at[q, a * nb + b]
        return pltpu.make_async_copy(kept.at[a * nb + b], target, local.at[which, r])

    def turn_arrival(f):
        return pltpu.make_async_copy(turned.at[f], turned.at[f], recv_turn.at[f])

    barrier = pltpu.get_barrier_semaphore()

    def greet(layer, core, column):
        pl.semaphore_signal(barrier, inc=1, device_id=device(layer, core, column), device_id_type=MESH)

    for column in range(layers):
        greet(z, 1 - c, column)

        @pl.when(column != q)
        def _():
            greet(z, c, column)

    @pl.when(z > 0)
    def _():
        greet(z - 1, c, q)

    @pl.when(z < layers - 1)
    def _():
        greet(z + 1, c, q)

    ends = jnp.where(z > 0, 1, 0) + jnp.where(z < layers - 1, 1, 0)
    pl.semaphore_wait(barrier, 2 * layers - 1 + ends)

    def own_moves(r, do):
        @pl.when(z > 0)
        def _():
            do(move(DOWN, z, r, kept))

        @pl.when(z < layers - 1)
        def _():
            do(move(UP, z, r, kept))

        do(move(SIDE, z, r, kept))
        for other in range(layers):

            @pl.when((other != q) & ((other % int_count == x) | (other // int_count == y)))
            def _():
                do(row_send(other, r))

    def start(copy):
        copy.start()

    def own_round(r):
        a, b = place(z, q, r)

        square = a * nb + b

        @pl.when(z > q)
        def _():
            kept[square] = own[square]

        @pl.when(z <= q)
        def _():
            turn_arrival(r).wait()
            per = edge // TILE
            lanes = pl.ds(pl.multiple_of(b * edge, edge), edge)
            for comp in range(2):
                flipped = turned[r, comp].T
                for i in range(per):
                    row = slice(i * TILE, (i + 1) * TILE)
                    marks = mask[pl.ds(pl.multiple_of((a * per + i) * 8, 8), 1), lanes]
                    kept[square, comp, row] = jnp.where(marks > 0.5, flipped[row], own[square, comp, row])

        own_moves(r, start)
        keep(0, r).start()
        keep(1, r).start()

    def pass_on(j, r, do, waiting):
        @pl.when(z < j)
        def _():
            if waiting:
                arrival(DOWN, j, c, r).wait_recv()

            @pl.when(z > 0)
            def _():
                do(move(DOWN, j, r, None))

            @pl.when(q == z)
            def _():
                do(turn(j, r, None))

        @pl.when(z > j)
        def _():
            if waiting:
                arrival(UP, j, c, r).wait_recv()

            @pl.when(z < layers - 1)
            def _():
                do(move(UP, j, r, None))

        @pl.when(z != j)
        def _():
            do(move(SIDE, j, r, None))

    def first_turn(r, _):
        @pl.when(straight(r)[1] // na == c)
        def _():
            turn_here(r).start()

        @pl.when(straight(r)[1] // na != c)
        def _():
            turn(z, r, own).start()

        return 0

    @pl.when(q == z)
    def _():
        lax.fori_loop(0, rounds, first_turn, 0)

    def step(t, _):
        @pl.when((t < rounds) & (z > q))
        def _():
            own_round(t)

        @pl.when(t < rounds)
        def _():
            for j in range(layers):

                @pl.when(j > q)
                def _():
                    pass_on(j, t, start, True)

        @pl.when((t >= LAG_FILL) & (t < rounds + LAG_FILL) & (z <= q))
        def _():
            own_round(t - LAG_FILL)

        @pl.when(t >= LAG_MOVE)
        def _():
            for j in range(layers):

                @pl.when(j <= q)
                def _():
                    pass_on(j, t - LAG_MOVE, start, True)

            relays(t - LAG_MOVE, start, True)

        return 0

    lax.fori_loop(0, rounds + LAG_MOVE, step, 0)

    def done(copy):
        copy.wait_send()

    def finish(r, _):
        own_moves(r, done)
        relays(r, done, False)
        keep(0, r).wait()
        keep(1, r).wait()
        for j in range(layers):
            pass_on(j, r, done, False)
            arrival(SIDE, j, 1 - c, r).wait_recv()

            @pl.when((j != q) & (j % int_count != x))
            def _():
                row_arrival(j, r).wait_recv()

        @pl.when((q == z) & (straight(r)[1] // na != c))
        def _():
            turn(z, r, own).wait_send()

        return 0

    lax.fori_loop(0, rounds, finish, 0)


def gather_panels(own, mask, layers, int_count):
    rounds, _, edge, _ = own.shape
    rows = edge * int((rounds // 2) ** 0.5)
    return pl.pallas_call(
        functools.partial(gather_kernel, (layers, int_count, rows, edge)),
        out_shape=(
            jax.ShapeDtypeStruct((2 * layers, *own.shape), jnp.float32),
            jax.ShapeDtypeStruct((layers, *own.shape), jnp.float32),
        ),
        in_specs=[pl.BlockSpec(memory_space=pltpu.VMEM)] * 2,
        out_specs=[pl.BlockSpec(memory_space=pl.ANY)] * 2,
        scratch_shapes=[
            pltpu.VMEM(own.shape, jnp.float32),
            pltpu.VMEM(own.shape, jnp.float32),
            pltpu.SemaphoreType.DMA((4, layers, rounds)),
            pltpu.SemaphoreType.DMA((rounds,)),
            pltpu.SemaphoreType.DMA((6, layers, rounds)),
            pltpu.SemaphoreType.DMA((2, rounds)),
        ],
        compiler_params=pltpu.CompilerParams(
            collective_id=0, has_side_effects=True, vmem_limit_bytes=40 * 2**20
        ),
    )(own, mask)


def per_device(traces, missing, aperture, wavelet):
    src_count, rcv_count, int_count = (lax.axis_size(a) for a in EVERY)
    col_count = rcv_count * int_count
    assert src_count == 2 * col_count
    rows, wide = traces.shape[2], traces.shape[3]
    cols = wide // int_count
    my_int = lax.axis_index("int")
    s = lax.axis_index("src")
    own = lax.dynamic_slice_in_dim(traces[:, 0], my_int * cols, cols, axis=2)
    row_tiles, col_tiles = rows // TILE, cols // TILE
    my_missing = lax.dynamic_slice_in_dim(missing, my_int * col_tiles, col_tiles, axis=1)
    mask = jnp.repeat(jnp.repeat((my_missing > 0).astype(jnp.float32), 8, axis=0), TILE, axis=1)
    edge = max(TILE, rows // 4)
    na = rows // edge
    own = jnp.stack(
        [own[:, a * edge : (a + 1) * edge, b * edge : (b + 1) * edge] for a in range(na) for b in range(2 * na)]
    )
    right, left = gather_panels(own, mask, col_count, int_count)
    blocks = col_count * col_tiles
    chosen = (
        (aperture[:, :, None] == jnp.arange(blocks, dtype=jnp.int32)[None, None, :])
        .astype(jnp.float32)
        .sum(axis=1)
    )
    return predict(left, right, chosen, wavelet, s.reshape(1), na)[:, None]


def solution(mesh):
    placed = (P(None, None, "src", "rcv"), P("src", "rcv"), P("src", None), P())
    return jax.shard_map(
        per_device,
        mesh=mesh,
        in_specs=placed,
        out_specs=P(None, None, "src", ("rcv", "int")),
        check_vma=False,
    )
```

```python
import functools

import jax
import jax.numpy as jnp
from jax import lax
from jax.experimental import pallas as pl
from jax.experimental.pallas import tpu as pltpu
from jax.sharding import PartitionSpec as P

TILE = 128
EVERY = ("src", "rcv", "int")
MESH = pl.DeviceIdType.MESH
LAG_FILL = 2
LAG_MOVE = 3


def split(value):
    high = value.astype(jnp.bfloat16)
    return high, (value - high.astype(jnp.float32)).astype(jnp.bfloat16)


def three_pass(left_parts, right_parts):
    (lh, ll), (rh, rl) = left_parts, right_parts
    dot = functools.partial(jnp.dot, preferred_element_type=jnp.float32)
    return dot(lh, rh) + (dot(lh, rl) + dot(ll, rh))


def predict_kernel(my_block, left, right, chosen, kept, wavelet, out, total):
    step = pl.program_id(1)
    na, _, _, edge, _ = left.shape
    nb = right.shape[1]
    per = edge // TILE

    @pl.when(step == 0)
    def _():
        total[...] = jnp.zeros_like(total)

    def weighted(comp):
        bands = []
        for a in range(na):
            for i in range(per):
                tiles = []
                for b in range(na):
                    for k in range(per):
                        tile = left[a, b, comp, i * TILE : (i + 1) * TILE, k * TILE : (k + 1) * TILE]
                        tiles.append(tile * chosen[a * per + i, (step * na + b) * per + k])
                bands.append(jnp.concatenate(tiles, axis=1))
        return jnp.concatenate(bands, axis=0)

    def panel(comp):
        bands = [jnp.concatenate([right[a, b, comp] for b in range(nb)], axis=1) for a in range(na)]
        return jnp.concatenate(bands, axis=0)

    lr, li = weighted(0), weighted(1)
    fr, fi = panel(0), panel(1)
    first = three_pass(split(lr), split(fr))
    second = three_pass(split(li), split(fi))
    total[0] += first - second
    total[1] += three_pass(split(lr + li), split(fr + fi)) - (first + second)

    @pl.when(step == pl.num_programs(1) - 1)
    def _():
        wr, wi = wavelet[0, 0], wavelet[1, 0]
        for a in range(na):
            for b in range(nb):
                at = (slice(a * edge, (a + 1) * edge), slice(b * edge, (b + 1) * edge))
                real, imag = total[0, *at], total[1, *at]
                out[0, *at] = kept[a, b, 0] - (wr * real - wi * imag)
                out[1, *at] = kept[a, b, 1] - (wr * imag + wi * real)


def predict(left, right, chosen, wavelet, my_block, na):
    columns, rounds, _, edge, _ = left.shape
    blocks = right.shape[0]
    nb = rounds // na
    left = left.reshape(columns, na, nb, 2, edge, edge)
    right = right.reshape(blocks, na, nb, 2, edge, edge)
    rows, cols = na * edge, nb * edge
    width = min(cols, 512)
    some = width // edge
    panel = (None, na, some, 2, edge, edge)
    return pl.pallas_call(
        predict_kernel,
        grid_spec=pltpu.PrefetchScalarGridSpec(
            num_scalar_prefetch=1,
            grid=(cols // width, blocks),
            in_specs=[
                pl.BlockSpec((None, na, na, 2, edge, edge), lambda n, k, s: (k // 2, 0, k % 2, 0, 0, 0)),
                pl.BlockSpec(panel, lambda n, k, s: (k, 0, n, 0, 0, 0)),
                pl.BlockSpec(memory_space=pltpu.SMEM),
                pl.BlockSpec(panel, lambda n, k, s: (s[0], 0, n, 0, 0, 0)),
                pl.BlockSpec(memory_space=pltpu.SMEM),
            ],
            out_specs=pl.BlockSpec((2, rows, width), lambda n, k, s: (0, 0, n)),
            scratch_shapes=[pltpu.VMEM((2, rows, width), jnp.float32)],
        ),
        out_shape=jax.ShapeDtypeStruct((2, rows, cols), jnp.float32),
        compiler_params=pltpu.CompilerParams(vmem_limit_bytes=56 * 2**20),
    )(my_block, left, right, chosen, right, wavelet)


def gather_kernel(sizes, own, mask, right, left, turned, kept, recv, recv_turn, sent, local):
    layers, int_count, rows, edge = sizes
    na = rows // edge
    nb = 2 * na
    rounds = na * nb
    s = lax.axis_index("src")
    z, c = s // 2, s % 2
    y, x = lax.axis_index("rcv"), lax.axis_index("int")
    q = y * int_count + x

    def device(layer, core, column):
        return {"src": 2 * layer + core, "rcv": column // int_count, "int": column % int_count}

    def straight(r):
        a, rest = r // nb, r % nb
        return a, na * (rest % 2) + rest // 2

    def mirrored(r):
        a, rest = r // nb, r % nb
        return rest // 2, na * (rest % 2) + a

    def place(layer, column, r):
        (a0, b0), (a1, b1) = straight(r), mirrored(r)
        raw = jnp.where(layer > column, 1, 0)
        return a0 * raw + a1 * (1 - raw), b0 * raw + b1 * (1 - raw)

    def in_right(layer, core, a, b):
        return right.at[2 * layer + core, a * nb + b]

    DOWN, UP, SIDE, ROW, TURN, RELAY, FAR = range(7)
    last = layers - 1
    assert last > 1

    def remote(source, target, kind, j, r, where, sem=None):
        return pltpu.make_async_remote_copy(
            src_ref=source,
            dst_ref=target,
            send_sem=sent.at[kind, j, r],
            recv_sem=recv.at[kind, j, r] if sem is None else sem,
            device_id=where,
            device_id_type=MESH,
        )

    def move(kind, j, r, source):
        a, b = place(j, q, r)
        where = {DOWN: (z - 1, c), UP: (z + 1, c), SIDE: (z, 1 - c)}[kind]
        source = in_right(j, c, a, b) if source is None else source.at[a * nb + b]
        return remote(source, in_right(j, c, a, b), kind, j, r, device(*where, q))

    def far_move(to, kind, r):
        a, b = place(z, q, r)
        target = in_right(z, c, a, b)
        return remote(kept.at[a * nb + b], target, FAR, z, r, device(to, c, q), recv.at[kind, z, r])

    def arrival(kind, j, core, r):
        a, b = place(j, q, r)
        ref = in_right(j, core, a, b)
        return remote(ref, ref, kind, j, r, device(z, 1 - c, q))

    def row_send(other, r):
        a, b = place(z, q, r)
        return remote(
            kept.at[a * nb + b], left.at[q, a * nb + b], ROW, other, r, device(z, c, other),
            recv.at[ROW, q, r],
        )

    def row_arrival(other, r):
        a, b = place(z, other, r)
        ref = left.at[other, a * nb + b]
        return remote(ref, ref, ROW, other, r, device(z, 1 - c, q))

    def relays(r, do, waiting):
        for other in range(layers):

            @pl.when((other != q) & (other % int_count == x))
            def _():
                if waiting:
                    row_arrival(other, r).wait_recv()
                a, b = place(z, other, r)
                ref = left.at[other, a * nb + b]
                for x2 in range(int_count):

                    @pl.when(x2 != x)
                    def _():
                        to = (other // int_count) * int_count + x2
                        where = device(z, c, y * int_count + x2)
                        do(remote(ref, ref, RELAY, to, r, where, recv.at[ROW, other, r]))

    def turn_parts(j, r, source):
        a, b = straight(r)
        core = b // na
        slot = a * nb + 2 * (b % na) + c
        ref = in_right(j, c, a, b) if source is None else source.at[a * nb + b]
        return ref, core, slot

    def turn(j, r, source):
        ref, core, slot = turn_parts(j, r, source)
        return remote(ref, turned.at[slot], TURN, j, r, device(z, core, j), recv_turn.at[slot])

    def turn_here(r):
        ref, _, slot = turn_parts(z, r, own)
        return pltpu.make_async_copy(ref, turned.at[slot], recv_turn.at[slot])

    def keep(which, r):
        a, b = place(z, q, r)
        target = in_right(z, c, a, b) if which == 0 else left.at[q, a * nb + b]
        return pltpu.make_async_copy(kept.at[a * nb + b], target, local.at[which, r])

    def turn_arrival(f):
        return pltpu.make_async_copy(turned.at[f], turned.at[f], recv_turn.at[f])

    barrier = pltpu.get_barrier_semaphore()

    def greet(layer, core, column):
        pl.semaphore_signal(barrier, inc=1, device_id=device(layer, core, column), device_id_type=MESH)

    for column in range(layers):
        greet(z, 1 - c, column)

        @pl.when(column != q)
        def _():
            greet(z, c, column)

    @pl.when(z > 0)
    def _():
        greet(z - 1, c, q)

    @pl.when(z < layers - 1)
    def _():
        greet(z + 1, c, q)

    @pl.when(z == 0)
    def _():
        greet(last, c, q)

    @pl.when(z == last)
    def _():
        greet(0, c, q)

    pl.semaphore_wait(barrier, 2 * layers + 1)

    def own_moves(r, do):
        @pl.when(z > 0)
        def _():
            do(move(DOWN, z, r, kept))

        @pl.when(z < layers - 1)
        def _():
            do(move(UP, z, r, kept))

        @pl.when(z == 0)
        def _():
            do(far_move(last, UP, r))

        @pl.when(z == last)
        def _():
            do(far_move(0, DOWN, r))

        do(move(SIDE, z, r, kept))
        for other in range(layers):

            @pl.when((other != q) & ((other % int_count == x) | (other // int_count == y)))
            def _():
                do(row_send(other, r))

    def start(copy):
        copy.start()

    def own_round(r):
        a, b = place(z, q, r)

        square = a * nb + b

        @pl.when(z > q)
        def _():
            kept[square] = own[square]

        @pl.when(z <= q)
        def _():
            turn_arrival(r).wait()
            per = edge // TILE
            lanes = pl.ds(pl.multiple_of(b * edge, edge), edge)
            for comp in range(2):
                flipped = turned[r, comp].T
                for i in range(per):
                    row = slice(i * TILE, (i + 1) * TILE)
                    marks = mask[pl.ds(pl.multiple_of((a * per + i) * 8, 8), 1), lanes]
                    kept[square, comp, row] = jnp.where(marks > 0.5, flipped[row], own[square, comp, row])

        own_moves(r, start)
        keep(0, r).start()
        keep(1, r).start()

    def pass_on(j, r, do, waiting):
        @pl.when(z < j)
        def _():
            if waiting:
                arrival(DOWN, j, c, r).wait_recv()

            @pl.when((z > 1) | ((z > 0) & (j < last)))
            def _():
                do(move(DOWN, j, r, None))

            @pl.when(q == z)
            def _():
                do(turn(j, r, None))

        @pl.when(z > j)
        def _():
            if waiting:
                arrival(UP, j, c, r).wait_recv()

            @pl.when((z < last - 1) | ((z < last) & (j > 0)))
            def _():
                do(move(UP, j, r, None))

        @pl.when(z != j)
        def _():
            do(move(SIDE, j, r, None))

    def first_turn(r, _):
        @pl.when(straight(r)[1] // na == c)
        def _():
            turn_here(r).start()

        @pl.when(straight(r)[1] // na != c)
        def _():
            turn(z, r, own).start()

        return 0

    @pl.when(q == z)
    def _():
        lax.fori_loop(0, rounds, first_turn, 0)

    def step(t, _):
        @pl.when((t < rounds) & (z > q))
        def _():
            own_round(t)

        @pl.when(t < rounds)
        def _():
            for j in range(layers):

                @pl.when(j > q)
                def _():
                    pass_on(j, t, start, True)

        @pl.when((t >= LAG_FILL) & (t < rounds + LAG_FILL) & (z <= q))
        def _():
            own_round(t - LAG_FILL)

        @pl.when(t >= LAG_MOVE)
        def _():
            for j in range(layers):

                @pl.when(j <= q)
                def _():
                    pass_on(j, t - LAG_MOVE, start, True)

            relays(t - LAG_MOVE, start, True)

        return 0

    lax.fori_loop(0, rounds + LAG_MOVE, step, 0)

    def done(copy):
        copy.wait_send()

    def finish(r, _):
        own_moves(r, done)
        relays(r, done, False)
        keep(0, r).wait()
        keep(1, r).wait()
        for j in range(layers):
            pass_on(j, r, done, False)
            arrival(SIDE, j, 1 - c, r).wait_recv()

            @pl.when((j != q) & (j % int_count != x))
            def _():
                row_arrival(j, r).wait_recv()

        @pl.when((q == z) & (straight(r)[1] // na != c))
        def _():
            turn(z, r, own).wait_send()

        return 0

    lax.fori_loop(0, rounds, finish, 0)


def gather_panels(own, mask, layers, int_count):
    rounds, _, edge, _ = own.shape
    rows = edge * int((rounds // 2) ** 0.5)
    return pl.pallas_call(
        functools.partial(gather_kernel, (layers, int_count, rows, edge)),
        out_shape=(
            jax.ShapeDtypeStruct((2 * layers, *own.shape), jnp.float32),
            jax.ShapeDtypeStruct((layers, *own.shape), jnp.float32),
        ),
        in_specs=[pl.BlockSpec(memory_space=pltpu.VMEM)] * 2,
        out_specs=[pl.BlockSpec(memory_space=pl.ANY)] * 2,
        scratch_shapes=[
            pltpu.VMEM(own.shape, jnp.float32),
            pltpu.VMEM(own.shape, jnp.float32),
            pltpu.SemaphoreType.DMA((4, layers, rounds)),
            pltpu.SemaphoreType.DMA((rounds,)),
            pltpu.SemaphoreType.DMA((7, layers, rounds)),
            pltpu.SemaphoreType.DMA((2, rounds)),
        ],
        compiler_params=pltpu.CompilerParams(
            collective_id=0, has_side_effects=True, vmem_limit_bytes=40 * 2**20
        ),
    )(own, mask)


def per_device(traces, missing, aperture, wavelet):
    src_count, rcv_count, int_count = (lax.axis_size(a) for a in EVERY)
    col_count = rcv_count * int_count
    assert src_count == 2 * col_count
    rows, wide = traces.shape[2], traces.shape[3]
    cols = wide // int_count
    my_int = lax.axis_index("int")
    s = lax.axis_index("src")
    own = lax.dynamic_slice_in_dim(traces[:, 0], my_int * cols, cols, axis=2)
    row_tiles, col_tiles = rows // TILE, cols // TILE
    my_missing = lax.dynamic_slice_in_dim(missing, my_int * col_tiles, col_tiles, axis=1)
    mask = jnp.repeat(jnp.repeat((my_missing > 0).astype(jnp.float32), 8, axis=0), TILE, axis=1)
    edge = max(TILE, rows // 2)
    na = rows // edge
    own = jnp.stack(
        [own[:, a * edge : (a + 1) * edge, b * edge : (b + 1) * edge] for a in range(na) for b in range(2 * na)]
    )
    right, left = gather_panels(own, mask, col_count, int_count)
    blocks = col_count * col_tiles
    chosen = (
        (aperture[:, :, None] == jnp.arange(blocks, dtype=jnp.int32)[None, None, :])
        .astype(jnp.float32)
        .sum(axis=1)
    )
    return predict(left, right, chosen, wavelet, s.reshape(1), na)[:, None]


def solution(mesh):
    placed = (P(None, None, "src", "rcv"), P("src", "rcv"), P("src", None), P())
    return jax.shard_map(
        per_device,
        mesh=mesh,
        in_specs=placed,
        out_specs=P(None, None, "src", ("rcv", "int")),
        check_vma=False,
    )
```
